32 devices in a mesh: chain: 4 (over y, x), row: 8 (over z, core).
Axes of the slice: x: 2, y: 2, z: 4, core: 2. Of those that a mesh axis runs over, the one named last changes fastest.
Arguments:
- right_side: float32 [131072, 128], P('row'), may hold values from -6 to 6
- factor: bfloat16 [131072, 1, 2048], P('row', None, 'chain'), may hold values from -0.125 to 0.125
- tile_scales: float32 [256, 1, 4], P('row', None, 'chain'), may hold values from 0.5 to 2
- diag_inverse: float32 [1, 512, 2048], P(None, None, 'chain'), may hold values from -0.25 to 0.25
Outputs:
- updated: float32 [131072, 128], P('row')
The draws below stay inside these ranges and needn't reach their ends.
All inputs are finite; a program needn't handle non-finite values.
Results may differ from the reference program's by a relative error of at most 0.0031.
Values may be sent and summed in bfloat16 or wider, within the bound.
A program may use at most 128 MiB of HBM per device.

```python
import math
import jax
import jax.numpy as jnp
from jax import lax

N = 131072
RHS = 128
NB = 512
ROUNDS = 1
WINDOW = 2048
CHAIN_COLS = 2048
N_CHAIN = 4


def level_of(key, extent, cuts, low, largest):
    gain, own = 1.0, jax.random.fold_in(key, 6)
    for axis_at, shards_of in cuts:
        draws = jnp.exp(jax.random.uniform(jax.random.fold_in(own, axis_at), (shards_of,), jnp.float32, low / len(cuts), largest / len(cuts)))
        gain = gain * jnp.repeat(draws, extent[axis_at] // shards_of).reshape([-1 if axis == axis_at else 1 for axis in range(len(extent))])
    return gain


def gaussian(own_key, dims, spread, limit, cuts=(), kind=jnp.bfloat16):
    array = spread * jax.random.normal(own_key, dims, jnp.float32)
    if cuts:
        array = array * level_of(own_key, dims, cuts, -0.22, 0.18)
    return jnp.clip(array, -limit, limit).astype(kind)


def setup_inputs(seed: int = 0) -> dict:
    keys = jax.random.split(jax.random.key(seed), 5)
    return {
        "right_side": gaussian(keys[0], (N, RHS), 1.0, 6.0, ((0, 8),), jnp.float32),
        "factor": gaussian(keys[1], (N, ROUNDS, CHAIN_COLS), WINDOW ** -0.5, 0.125, ((0, 8), (2, 4))),
        "tile_scales": jnp.clip(jnp.exp(math.log(2.0) - 1.3862944 * jax.random.uniform(keys[2], (N // NB, ROUNDS, N_CHAIN), jnp.float32) ** level_of(keys[2], (N // NB, ROUNDS, N_CHAIN), ((0, 8), (2, 4)), -0.2, 0.2)), 0.5, 2.0),
        "diag_inverse": gaussian(keys[3], (ROUNDS, NB, CHAIN_COLS), NB ** -0.5, 0.25, ((2, 4),), jnp.float32),
    }


def reference(right_side, factor, tile_scales, diag_inverse):
    row_count, rhs_count = right_side.shape
    block_count = ROUNDS * N_CHAIN
    window = block_count * NB
    row_ids = jnp.arange(row_count, dtype=jnp.int32)
    zero = jnp.int32(0)

    def step(column, carry):
        carried, solved = carry
        column = jnp.asarray(column).astype(jnp.int32)
        round_index = column // N_CHAIN
        chain_slot = column % N_CHAIN
        block_start = column * NB
        residue = lax.dynamic_slice(right_side, (block_start, zero), (NB, rhs_count)) - lax.dynamic_slice(carried, (block_start, zero), (NB, rhs_count))
        inverse = lax.dynamic_slice(diag_inverse, (round_index, zero, chain_slot * NB), (1, NB, NB))[0]
        solved_now = jnp.dot(inverse, residue, precision=lax.Precision.HIGHEST, preferred_element_type=jnp.float32)
        solved_low = solved_now.astype(jnp.bfloat16)
        panel = lax.dynamic_slice(factor, (zero, round_index, chain_slot * NB), (row_count, 1, NB))[:, 0, :]
        product = jnp.dot(panel.astype(jnp.float32), solved_low.astype(jnp.float32), precision=lax.Precision.HIGHEST, preferred_element_type=jnp.float32)
        tile_scale = lax.dynamic_slice(tile_scales, (zero, round_index, chain_slot), (row_count // NB, 1, 1))[:, 0, 0]
        product = (product.reshape(row_count // NB, NB, rhs_count) * tile_scale[:, None, None]).reshape(row_count, rhs_count)
        below = row_ids >= block_start + NB
        carried = carried + jnp.where(below[:, None], product, jnp.zeros_like(product))
        solved = lax.dynamic_update_slice(solved, solved_now, (block_start, zero))
        return carried, solved

    carried = jnp.zeros((row_count, rhs_count), jnp.float32)
    solved = jnp.zeros((window, rhs_count), jnp.float32)
    carried, solved = lax.fori_loop(0, block_count, step, (carried, solved))
    tail = right_side[window:] - carried[window:]
    return jnp.concatenate([solved, tail], axis=0)
```

```python
import functools

import jax
import jax.numpy as jnp
from jax import lax
from jax.experimental import pallas as pl
from jax.experimental.pallas import tpu as pltpu
from jax.sharding import PartitionSpec as P

MESH = pl.DeviceIdType.MESH
SUB = 2


def kernel(chains, rows, rhs_ref, fac_ref, scale_ref, inv_ref, out_ref,
           fac, acc, inv, res, low, con_out, con_in, rel_out, dir_out, cmb_out, rel_in, dir_in, cmb_in, own,
           load_sem, xs_send, x_recv, cs_send, c_recv,
           rel_s, rel_r, dir_s, dir_r, cmb_s, cmb_r, ag_s, ag_r, fw_s, fw_r, own_sem):
    me = lax.axis_index("chain")
    row = lax.axis_index("row")
    local_rows, width = fac.shape
    tile = width
    window = chains * tile
    quarter = local_rows // 4
    half = quarter // 2
    piece = half // SUB
    peer = (me + 1 - 2 * (me % 2), me + 2 - 4 * (me // 2))
    across = 3 - me

    first = pltpu.make_async_copy(fac_ref.at[pl.ds(0, window)], fac.at[pl.ds(0, window)], load_sem.at[0])
    inv_load = pltpu.make_async_copy(inv_ref, inv, load_sem.at[1])
    own_load = pltpu.make_async_copy(rhs_ref.at[pl.ds(me * quarter, quarter)], acc, load_sem.at[2])
    res_load = pltpu.make_async_copy(rhs_ref.at[pl.ds(me * tile, tile)], res, load_sem.at[3])
    rest = None
    if local_rows > window:
        rest = pltpu.make_async_copy(
            fac_ref.at[pl.ds(window, local_rows - window)],
            fac.at[pl.ds(window, local_rows - window)], load_sem.at[4])

    @pl.when(row == 0)
    def _():
        inv_load.start()
        res_load.start()

    first.start()

    barrier = pltpu.get_barrier_semaphore()

    def greet(chain_to, row_to):
        pl.semaphore_signal(barrier, inc=1, device_id={"chain": chain_to, "row": row_to}, device_id_type=MESH)

    for hop in range(1, chains):
        greet(lax.rem(me + hop, chains), row)
    heads = [r for r in range(2, rows, 2)] + [1]

    @pl.when(row == 0)
    def _():
        for r in heads:
            greet(me, r)
        pl.semaphore_wait(barrier, chains - 1 + len(heads))

    @pl.when((row > 0) & (row % 2 == 0))
    def _():
        greet(me, 0)
        greet(me, row + 1)
        pl.semaphore_wait(barrier, chains - 1 + 2)

    @pl.when(row % 2 == 1)
    def _():
        greet(me, row - 1)
        pl.semaphore_wait(barrier, chains - 1 + 1)

    if rest is not None:
        rest.start()
    own_load.start()

    def send_low(row_to, sem):
        return pltpu.make_async_remote_copy(
            src_ref=low, dst_ref=low, send_sem=xs_send.at[sem], recv_sem=x_recv,
            device_id={"chain": me, "row": row_to}, device_id_type=MESH)

    def send_con(chain_to):
        return pltpu.make_async_remote_copy(
            src_ref=con_out.at[chain_to], dst_ref=con_in.at[me], send_sem=cs_send.at[chain_to],
            recv_sem=c_recv.at[me], device_id={"chain": chain_to, "row": row}, device_id_type=MESH)

    def recv_con(source):
        return pltpu.make_async_remote_copy(
            src_ref=con_out.at[source], dst_ref=con_in.at[source], send_sem=cs_send.at[source],
            recv_sem=c_recv.at[source], device_id={"chain": source, "row": row}, device_id_type=MESH)

    first.wait()

    @pl.when(row == 0)
    def _():
        inv_load.wait()
        res_load.wait()
        for j in range(chains - 1):
            @pl.when(j < me)
            def _():
                recv_con(j).wait_recv()
                res[...] = res[...] - con_in[j]
        solved = jnp.dot(inv[...], res[...], precision=lax.Precision.HIGHEST,
                         preferred_element_type=jnp.float32)
        low[...] = solved.astype(jnp.bfloat16)
        for i in range(1, chains):
            @pl.when(i > me)
            def _():
                con_out[i] = scale_ref[i] * jnp.dot(
                    fac[pl.ds(i * tile, tile), :], low[...], preferred_element_type=jnp.float32)
                send_con(i).start()
        for at, r in enumerate(heads):
            send_low(r, at).start()

    @pl.when(row > 0)
    def _():
        send_low(0, 0).wait_recv()

    @pl.when((row > 0) & (row % 2 == 0))
    def _():
        send_low(row + 1, 0).start()

    if rest is not None:
        rest.wait()
    own_load.wait()

    step = min(piece, tile)

    def partial(start, put):
        def body(t, carry):
            at = pl.multiple_of(start + t * step, step)
            index = at // tile
            value = scale_ref[index] * jnp.dot(fac[pl.ds(at, step), :], low[...], preferred_element_type=jnp.float32)
            put(t * step, value)

            @pl.when((row == 0) & (at < window))
            def _():
                keep = jnp.where(index == me, -1.0, 0.0)
                put(t * step, keep * low[pl.ds(at - index * tile, step), :].astype(jnp.float32))
            return carry
        lax.fori_loop(0, piece // step, body, 0)

    def putter(ref, a, s):
        def put(offset, value):
            ref[a, s, pl.ds(offset, step), :] = value.astype(jnp.bfloat16)
        return put

    def message(src, dst, send, recv, a, s):
        return pltpu.make_async_remote_copy(
            src_ref=src.at[a, s], dst_ref=dst.at[a, s], send_sem=send.at[a, s], recv_sem=recv.at[a, s],
            device_id={"chain": peer[a], "row": row}, device_id_type=MESH)

    def rel(a, s):
        return message(rel_out, rel_in, rel_s, rel_r, a, s)

    def direct(a, s):
        return message(dir_out, dir_in, dir_s, dir_r, a, s)

    def combined(a, s):
        return message(cmb_out, cmb_in, cmb_s, cmb_r, a, s)

    for s in range(SUB):
        for a in range(2):
            partial(across * quarter + (1 - a) * half + s * piece, putter(rel_out, a, s))
            rel(a, s).start()
    for s in range(SUB):
        for a in range(2):
            partial(peer[a] * quarter + (1 - a) * half + s * piece, putter(dir_out, a, s))
            direct(a, s).start()
    for s in range(SUB):
        for a in range(2):
            partial(peer[a] * quarter + a * half + s * piece, putter(cmb_out, a, s))

    @pl.when((row == 0) & (me * quarter < window))
    def _():
        masked = min(quarter, window)

        def wipe(t, carry):
            at = pl.multiple_of(t * step, step)

            @pl.when(me * quarter + at < window)
            def _():
                acc[pl.ds(at, step), :] = jnp.zeros((step, acc.shape[1]), jnp.float32)
            return carry
        lax.fori_loop(0, masked // step, wipe, 0)

    for h in range(2):
        for s in range(SUB):
            base = h * half + s * piece

            def body(t, carry, base=base):
                spot = pl.multiple_of(base + t * step, step)
                at = pl.multiple_of(me * quarter + spot, step)
                index = at // tile
                inside = (row == 0) & (at < window)

                @pl.when(jnp.logical_not(inside))
                def _():
                    acc[pl.ds(spot, step), :] -= scale_ref[index] * jnp.dot(
                        fac[pl.ds(at, step), :], low[...], preferred_element_type=jnp.float32)

                @pl.when(inside & (index == me))
                def _():
                    acc[pl.ds(spot, step), :] = low[pl.ds(at - index * tile, step), :].astype(jnp.float32)
                return carry
            lax.fori_loop(0, piece // step, body, 0)

    def where_is(block, h, s):
        return pl.ds(pl.multiple_of(block * quarter + h * half + s * piece, piece), piece)

    def spread(a, h, s):
        return pltpu.make_async_remote_copy(
            src_ref=own.at[h, s], dst_ref=out_ref.at[where_is(me, h, s)],
            send_sem=ag_s.at[a, h, s], recv_sem=ag_r.at[a, h, s],
            device_id={"chain": peer[a], "row": row}, device_id_type=MESH)

    def arrived(a, h, s):
        return pltpu.make_async_remote_copy(
            src_ref=own.at[h, s], dst_ref=out_ref.at[where_is(peer[a], h, s)],
            send_sem=ag_s.at[a, h, s], recv_sem=ag_r.at[a, h, s],
            device_id={"chain": peer[a], "row": row}, device_id_type=MESH)

    def forward(a, s):
        spot = out_ref.at[where_is(peer[a], a, s)]
        return pltpu.make_async_remote_copy(
            src_ref=spot, dst_ref=spot, send_sem=fw_s.at[a, s], recv_sem=fw_r.at[a, s],
            device_id={"chain": peer[1 - a], "row": row}, device_id_type=MESH)

    def forwarded(a, s):
        spot = out_ref.at[where_is(across, a, s)]
        return pltpu.make_async_remote_copy(
            src_ref=spot, dst_ref=spot, send_sem=fw_s.at[a, s], recv_sem=fw_r.at[a, s],
            device_id={"chain": peer[1 - a], "row": row}, device_id_type=MESH)

    def keep(h, s):
        return pltpu.make_async_copy(own.at[h, s], out_ref.at[where_is(me, h, s)], own_sem.at[h, s])

    for s in range(SUB):
        for a in range(2):
            rel(1 - a, s).wait_recv()
            cmb_out[a, s] = (cmb_out[a, s].astype(jnp.float32) + rel_in[1 - a, s].astype(jnp.float32)).astype(jnp.bfloat16)
            combined(a, s).start()
    for s in range(SUB):
        for h in range(2):
            direct(1 - h, s).wait_recv()
            combined(h, s).wait_recv()
            own[h, s] = (acc[pl.ds(h * half + s * piece, piece), :] - dir_in[1 - h, s].astype(jnp.float32)
                         - cmb_in[h, s].astype(jnp.float32)).astype(jnp.bfloat16)
            spread(h, h, s).start()
            spread(1 - h, h, s).start()
            keep(h, s).start()
    for s in range(SUB):
        for a in range(2):
            arrived(a, a, s).wait_recv()
            forward(a, s).start()
    for s in range(SUB):
        for a in range(2):
            arrived(a, 1 - a, s).wait_recv()
            forwarded(a, s).wait_recv()
            rel(a, s).wait_send()
            direct(a, s).wait_send()
            combined(a, s).wait_send()
            spread(a, 0, s).wait_send()
            spread(a, 1, s).wait_send()
            forward(a, s).wait_send()
            keep(a, s).wait()

    @pl.when(row == 0)
    def _():
        for i in range(1, chains):
            @pl.when(i > me)
            def _():
                send_con(i).wait_send()
        for at, r in enumerate(heads):
            send_low(r, at).wait_send()

    @pl.when((row > 0) & (row % 2 == 0))
    def _():
        send_low(row + 1, 0).wait_send()


def local(chains, rows, right_side, factor, tile_scales, diag_inverse):
    local_rows, rhs_count = right_side.shape
    width = factor.shape[2]
    factor = factor.reshape(local_rows, width)
    scales = tile_scales.reshape(-1)
    inverse = diag_inverse.reshape(width, width)
    half = local_rows // 8
    piece = half // SUB
    low = jnp.bfloat16
    pieces = pltpu.VMEM((2, SUB, piece, rhs_count), low)
    sems = pltpu.SemaphoreType.DMA((2, SUB))
    anywhere = pl.BlockSpec(memory_space=pl.ANY)
    heads = len(range(2, rows, 2)) + 1
    gathered = pl.pallas_call(
        functools.partial(kernel, chains, rows),
        out_shape=jax.ShapeDtypeStruct((local_rows, rhs_count), low),
        in_specs=[anywhere, anywhere, pl.BlockSpec(memory_space=pltpu.SMEM), anywhere],
        out_specs=anywhere,
        scratch_shapes=[
            pltpu.VMEM((local_rows, width), low),
            pltpu.VMEM((local_rows // 4, rhs_count), jnp.float32),
            pltpu.VMEM((width, width), jnp.float32),
            pltpu.VMEM((width, rhs_count), jnp.float32),
            pltpu.VMEM((width, rhs_count), low),
            pltpu.VMEM((chains, width, rhs_count), jnp.float32),
            pltpu.VMEM((chains, width, rhs_count), jnp.float32),
            pieces, pieces, pieces, pieces, pieces, pieces, pieces,
            pltpu.SemaphoreType.DMA((5,)),
            pltpu.SemaphoreType.DMA((heads,)),
            pltpu.SemaphoreType.DMA,
            pltpu.SemaphoreType.DMA((chains,)),
            pltpu.SemaphoreType.DMA((chains,)),
            sems, sems, sems, sems, sems, sems,
            pltpu.SemaphoreType.DMA((2, 2, SUB)),
            pltpu.SemaphoreType.DMA((2, 2, SUB)),
            sems, sems,
            sems,
        ],
        compiler_params=pltpu.CompilerParams(
            collective_id=0, has_side_effects=True, vmem_limit_bytes=48 * 2**20),
        cost_estimate=pl.CostEstimate(
            flops=2 * local_rows * width * rhs_count, bytes_accessed=2 * local_rows * width, transcendentals=0),
    )(right_side, factor, scales, inverse)
    return gathered.astype(jnp.float32)


def solution(mesh):
    return jax.shard_map(
        functools.partial(local, mesh.shape["chain"], mesh.shape["row"]),
        mesh=mesh,
        in_specs=(
            P("row", None),
            P("row", None, "chain"),
            P("row", None, "chain"),
            P(None, None, "chain"),
        ),
        out_specs=P("row", None),
        check_vma=False,
    )
```

```python
import functools

import jax
import jax.numpy as jnp
from jax import lax
from jax.experimental import pallas as pl
from jax.experimental.pallas import tpu as pltpu
from jax.sharding import PartitionSpec as P

MESH = pl.DeviceIdType.MESH
SUB = 4


def kernel(chains, rows, rhs_ref, fac_ref, scale_ref, inv_ref, out_ref,
           fac, acc, inv, inv_high, inv_low, res, low, con_out, con_in, rel_out, dir_out, cmb_out, rel_in, dir_in, cmb_in, own,
           load_sem, xs_send, x_recv, cs_send, c_recv,
           rel_s, rel_r, dir_s, dir_r, cmb_s, cmb_r, ag_s, ag_r, fw_s, fw_r, own_sem):
    me = lax.axis_index("chain")
    row = lax.axis_index("row")
    local_rows, width = fac.shape
    tile = width
    window = chains * tile
    quarter = local_rows // 4
    half = quarter // 2
    piece = half // SUB
    peer = (me + 1 - 2 * (me % 2), me + 2 - 4 * (me // 2))
    across = 3 - me

    first = pltpu.make_async_copy(fac_ref.at[pl.ds(0, window)], fac.at[pl.ds(0, window)], load_sem.at[0])
    inv_load = pltpu.make_async_copy(inv_ref, inv, load_sem.at[1])
    own_load = pltpu.make_async_copy(rhs_ref.at[pl.ds(me * quarter, quarter)], acc, load_sem.at[2])
    res_load = pltpu.make_async_copy(rhs_ref.at[pl.ds(me * tile, tile)], res, load_sem.at[3])
    rest = None
    if local_rows > window:
        rest = pltpu.make_async_copy(
            fac_ref.at[pl.ds(window, local_rows - window)],
            fac.at[pl.ds(window, local_rows - window)], load_sem.at[4])

    @pl.when(row == 0)
    def _():
        inv_load.start()
        res_load.start()

    first.start()

    barrier = pltpu.get_barrier_semaphore()

    def greet(chain_to, row_to):
        pl.semaphore_signal(barrier, inc=1, device_id={"chain": chain_to, "row": row_to}, device_id_type=MESH)

    for hop in range(1, chains):
        greet(lax.rem(me + hop, chains), row)
    heads = [r for r in range(2, rows, 2)][::-1] + [1]

    @pl.when(row == 0)
    def _():
        for r in heads:
            greet(me, r)
        pl.semaphore_wait(barrier, chains - 1 + len(heads))

    @pl.when((row > 0) & (row % 2 == 0))
    def _():
        greet(me, 0)
        greet(me, row + 1)
        pl.semaphore_wait(barrier, chains - 1 + 2)

    @pl.when(row % 2 == 1)
    def _():
        greet(me, row - 1)
        pl.semaphore_wait(barrier, chains - 1 + 1)

    if rest is not None:
        rest.start()
    own_load.start()

    def send_low(row_to, sem):
        return pltpu.make_async_remote_copy(
            src_ref=low, dst_ref=low, send_sem=xs_send.at[sem], recv_sem=x_recv,
            device_id={"chain": me, "row": row_to}, device_id_type=MESH)

    def send_con(chain_to):
        return pltpu.make_async_remote_copy(
            src_ref=con_out.at[chain_to], dst_ref=con_in.at[me], send_sem=cs_send.at[chain_to],
            recv_sem=c_recv.at[me], device_id={"chain": chain_to, "row": row}, device_id_type=MESH)

    def recv_con(source):
        return pltpu.make_async_remote_copy(
            src_ref=con_out.at[source], dst_ref=con_in.at[source], send_sem=cs_send.at[source],
            recv_sem=c_recv.at[source], device_id={"chain": source, "row": row}, device_id_type=MESH)

    first.wait()

    @pl.when(row == 0)
    def _():
        inv_load.wait()
        inv_high[...] = inv[...].astype(jnp.bfloat16)
        inv_low[...] = (inv[...] - inv_high[...].astype(jnp.float32)).astype(jnp.bfloat16)
        res_load.wait()
        for j in range(chains - 1):
            @pl.when(j < me)
            def _():
                recv_con(j).wait_recv()
                res[...] = res[...] - con_in[j]
        high = res[...].astype(jnp.bfloat16)
        rest_part = (res[...] - high.astype(jnp.float32)).astype(jnp.bfloat16)
        wide = jnp.dot(inv_high[...], jnp.concatenate([high, rest_part], axis=1),
                       preferred_element_type=jnp.float32)
        count = high.shape[1]
        solved = wide[:, :count] + (wide[:, count:] + jnp.dot(
            inv_low[...], high, preferred_element_type=jnp.float32))
        low[...] = solved.astype(jnp.bfloat16)
        for i in range(1, chains):
            @pl.when(i > me)
            def _():
                con_out[i] = scale_ref[i] * jnp.dot(
                    fac[pl.ds(i * tile, tile), :], low[...], preferred_element_type=jnp.float32)
                send_con(i).start()
        for at, r in enumerate(heads):
            send_low(r, at).start()

    @pl.when(row > 0)
    def _():
        send_low(0, 0).wait_recv()

    @pl.when((row > 0) & (row % 2 == 0))
    def _():
        send_low(row + 1, 0).start()

    if rest is not None:
        rest.wait()
    own_load.wait()

    step = min(piece, tile)

    def partial(start, put):
        def body(t, carry):
            at = pl.multiple_of(start + t * step, step)
            index = at // tile
            value = scale_ref[index] * jnp.dot(fac[pl.ds(at, step), :], low[...], preferred_element_type=jnp.float32)
            put(t * step, value)

            @pl.when((row == 0) & (at < window))
            def _():
                keep = jnp.where(index == me, -1.0, 0.0)
                put(t * step, keep * low[pl.ds(at - index * tile, step), :].astype(jnp.float32))
            return carry
        lax.fori_loop(0, piece // step, body, 0)

    def putter(ref, a, s):
        def put(offset, value):
            ref[a, s, pl.ds(offset, step), :] = value.astype(jnp.bfloat16)
        return put

    def message(src, dst, send, recv, a, s):
        return pltpu.make_async_remote_copy(
            src_ref=src.at[a, s], dst_ref=dst.at[a, s], send_sem=send.at[a, s], recv_sem=recv.at[a, s],
            device_id={"chain": peer[a], "row": row}, device_id_type=MESH)

    def rel(a, s):
        return message(rel_out, rel_in, rel_s, rel_r, a, s)

    def direct(a, s):
        return message(dir_out, dir_in, dir_s, dir_r, a, s)

    def combined(a, s):
        return message(cmb_out, cmb_in, cmb_s, cmb_r, a, s)

    for s in range(SUB):
        for a in range(2):
            partial(across * quarter + (1 - a) * half + s * piece, putter(rel_out, a, s))
            rel(a, s).start()
    for s in range(SUB):
        for a in range(2):
            partial(peer[a] * quarter + (1 - a) * half + s * piece, putter(dir_out, a, s))
            direct(a, s).start()
    for s in range(SUB):
        for a in range(2):
            partial(peer[a] * quarter + a * half + s * piece, putter(cmb_out, a, s))

    @pl.when((row == 0) & (me * quarter < window))
    def _():
        masked = min(quarter, window)

        def wipe(t, carry):
            at = pl.multiple_of(t * step, step)

            @pl.when(me * quarter + at < window)
            def _():
                acc[pl.ds(at, step), :] = jnp.zeros((step, acc.shape[1]), jnp.float32)
            return carry
        lax.fori_loop(0, masked // step, wipe, 0)

    for h in range(2):
        for s in range(SUB):
            base = h * half + s * piece

            def body(t, carry, base=base):
                spot = pl.multiple_of(base + t * step, step)
                at = pl.multiple_of(me * quarter + spot, step)
                index = at // tile
                inside = (row == 0) & (at < window)

                @pl.when(jnp.logical_not(inside))
                def _():
                    acc[pl.ds(spot, step), :] -= scale_ref[index] * jnp.dot(
                        fac[pl.ds(at, step), :], low[...], preferred_element_type=jnp.float32)

                @pl.when(inside & (index == me))
                def _():
                    acc[pl.ds(spot, step), :] = low[pl.ds(at - index * tile, step), :].astype(jnp.float32)
                return carry
            lax.fori_loop(0, piece // step, body, 0)

    def where_is(block, h, s):
        return pl.ds(pl.multiple_of(block * quarter + h * half + s * piece, piece), piece)

    def spread(a, h, s):
        return pltpu.make_async_remote_copy(
            src_ref=own.at[h, s], dst_ref=out_ref.at[where_is(me, h, s)],
            send_sem=ag_s.at[a, h, s], recv_sem=ag_r.at[a, h, s],
            device_id={"chain": peer[a], "row": row}, device_id_type=MESH)

    def arrived(a, h, s):
        return pltpu.make_async_remote_copy(
            src_ref=own.at[h, s], dst_ref=out_ref.at[where_is(peer[a], h, s)],
            send_sem=ag_s.at[a, h, s], recv_sem=ag_r.at[a, h, s],
            device_id={"chain": peer[a], "row": row}, device_id_type=MESH)

    def forward(a, h, s):
        spot = out_ref.at[where_is(peer[a], h, s)]
        return pltpu.make_async_remote_copy(
            src_ref=spot, dst_ref=spot, send_sem=fw_s.at[a, h, s], recv_sem=fw_r.at[a, h, s],
            device_id={"chain": peer[1 - a], "row": row}, device_id_type=MESH)

    def forwarded(a, h, s):
        spot = out_ref.at[where_is(across, h, s)]
        return pltpu.make_async_remote_copy(
            src_ref=spot, dst_ref=spot, send_sem=fw_s.at[a, h, s], recv_sem=fw_r.at[a, h, s],
            device_id={"chain": peer[1 - a], "row": row}, device_id_type=MESH)

    def forwards(a, h):
        return me < 3 if h == a else me == 0

    def is_forwarded(a, h):
        return me != 1 + a if h == a else me == 2 - a

    def keep(h, s):
        return pltpu.make_async_copy(own.at[h, s], out_ref.at[where_is(me, h, s)], own_sem.at[h, s])

    for s in range(SUB):
        for a in range(2):
            rel(1 - a, s).wait_recv()
            cmb_out[a, s] = (cmb_out[a, s].astype(jnp.float32) + rel_in[1 - a, s].astype(jnp.float32)).astype(jnp.bfloat16)
            combined(a, s).start()
    for s in range(SUB):
        for h in range(2):
            direct(1 - h, s).wait_recv()
            combined(h, s).wait_recv()
            own[h, s] = (acc[pl.ds(h * half + s * piece, piece), :] - dir_in[1 - h, s].astype(jnp.float32)
                         - cmb_in[h, s].astype(jnp.float32)).astype(jnp.bfloat16)
            spread(h, h, s).start()
            spread(1 - h, h, s).start()
            keep(h, s).start()
    halves = [(a, h) for h in range(2) for a in range(2)]
    for s in range(SUB):
        for a, h in halves:
            arrived(a, h, s).wait_recv()

            @pl.when(forwards(a, h))
            def _():
                forward(a, h, s).start()
    for s in range(SUB):
        for a, h in halves:
            @pl.when(is_forwarded(a, h))
            def _():
                forwarded(a, h, s).wait_recv()

            @pl.when(forwards(a, h))
            def _():
                forward(a, h, s).wait_send()
            spread(a, h, s).wait_send()
        for a in range(2):
            rel(a, s).wait_send()
            direct(a, s).wait_send()
            combined(a, s).wait_send()
            keep(a, s).wait()

    @pl.when(row == 0)
    def _():
        for i in range(1, chains):
            @pl.when(i > me)
            def _():
                send_con(i).wait_send()
        for at, r in enumerate(heads):
            send_low(r, at).wait_send()

    @pl.when((row > 0) & (row % 2 == 0))
    def _():
        send_low(row + 1, 0).wait_send()


def local(chains, rows, right_side, factor, tile_scales, diag_inverse):
    local_rows, rhs_count = right_side.shape
    width = factor.shape[2]
    factor = factor.reshape(local_rows, width)
    scales = tile_scales.reshape(-1)
    inverse = diag_inverse.reshape(width, width)
    half = local_rows // 8
    piece = half // SUB
    low = jnp.bfloat16
    pieces = pltpu.VMEM((2, SUB, piece, rhs_count), low)
    sems = pltpu.SemaphoreType.DMA((2, SUB))
    anywhere = pl.BlockSpec(memory_space=pl.ANY)
    heads = len(range(2, rows, 2)) + 1
    gathered = pl.pallas_call(
        functools.partial(kernel, chains, rows),
        out_shape=jax.ShapeDtypeStruct((local_rows, rhs_count), low),
        in_specs=[anywhere, anywhere, pl.BlockSpec(memory_space=pltpu.SMEM), anywhere],
        out_specs=anywhere,
        scratch_shapes=[
            pltpu.VMEM((local_rows, width), low),
            pltpu.VMEM((local_rows // 4, rhs_count), jnp.float32),
            pltpu.VMEM((width, width), jnp.float32),
            pltpu.VMEM((width, width), low),
            pltpu.VMEM((width, width), low),
            pltpu.VMEM((width, rhs_count), jnp.float32),
            pltpu.VMEM((width, rhs_count), low),
            pltpu.VMEM((chains, width, rhs_count), jnp.float32),
            pltpu.VMEM((chains, width, rhs_count), jnp.float32),
            pieces, pieces, pieces, pieces, pieces, pieces, pieces,
            pltpu.SemaphoreType.DMA((5,)),
            pltpu.SemaphoreType.DMA((heads,)),
            pltpu.SemaphoreType.DMA,
            pltpu.SemaphoreType.DMA((chains,)),
            pltpu.SemaphoreType.DMA((chains,)),
            sems, sems, sems, sems, sems, sems,
            pltpu.SemaphoreType.DMA((2, 2, SUB)),
            pltpu.SemaphoreType.DMA((2, 2, SUB)),
            pltpu.SemaphoreType.DMA((2, 2, SUB)),
            pltpu.SemaphoreType.DMA((2, 2, SUB)),
            sems,
        ],
        compiler_params=pltpu.CompilerParams(
            collective_id=0, has_side_effects=True, vmem_limit_bytes=48 * 2**20),
        cost_estimate=pl.CostEstimate(
            flops=2 * local_rows * width * rhs_count, bytes_accessed=2 * local_rows * width, transcendentals=0),
    )(right_side, factor, scales, inverse)
    return gathered.astype(jnp.float32)


def solution(mesh):
    return jax.shard_map(
        functools.partial(local, mesh.shape["chain"], mesh.shape["row"]),
        mesh=mesh,
        in_specs=(
            P("row", None),
            P("row", None, "chain"),
            P("row", None, "chain"),
            P(None, None, "chain"),
        ),
        out_specs=P("row", None),
        check_vma=False,
    )
```

```python
import functools

import jax
import jax.numpy as jnp
from jax import lax
from jax.experimental import pallas as pl
from jax.experimental.pallas import tpu as pltpu
from jax.sharding import PartitionSpec as P

MESH = pl.DeviceIdType.MESH
FLIGHT = 4
SUB = 4


def kernel(chains, rows, rhs_ref, fac_ref, scale_ref, inv_ref, out_ref,
           fac, acc, inv, inv_high, inv_low, res, low, con_out, con_in, rel_out, dir_out, cmb_out, rel_in, dir_in, cmb_in, own,
           load_sem, xs_send, x_recv, cs_send, c_recv,
           rel_s, rel_r, dir_s, dir_r, cmb_s, cmb_r, ag_s, ag_r, fw_s, fw_r, own_sem):
    me = lax.axis_index("chain")
    row = lax.axis_index("row")
    local_rows, width = fac.shape
    tile = width
    window = chains * tile
    quarter = local_rows // 4
    half = quarter // 2
    piece = half // SUB
    peer = (me + 1 - 2 * (me % 2), me + 2 - 4 * (me // 2))
    across = 3 - me

    first = pltpu.make_async_copy(fac_ref.at[pl.ds(0, window)], fac.at[pl.ds(0, window)], load_sem.at[0])
    inv_load = pltpu.make_async_copy(inv_ref, inv, load_sem.at[1])
    own_load = pltpu.make_async_copy(rhs_ref.at[pl.ds(me * quarter, quarter)], acc, load_sem.at[2])
    res_load = pltpu.make_async_copy(rhs_ref.at[pl.ds(me * tile, tile)], res, load_sem.at[3])
    rest = None
    if local_rows > window:
        rest = pltpu.make_async_copy(
            fac_ref.at[pl.ds(window, local_rows - window)],
            fac.at[pl.ds(window, local_rows - window)], load_sem.at[4])

    @pl.when(row == 0)
    def _():
        inv_load.start()
        res_load.start()

    first.start()

    barrier = pltpu.get_barrier_semaphore()

    def greet(chain_to, row_to):
        pl.semaphore_signal(barrier, inc=1, device_id={"chain": chain_to, "row": row_to}, device_id_type=MESH)

    for hop in range(1, chains):
        greet(lax.rem(me + hop, chains), row)
    heads = [r for r in range(2, rows, 2)][::-1] + [1]

    @pl.when(row == 0)
    def _():
        for r in heads:
            greet(me, r)
        pl.semaphore_wait(barrier, chains - 1 + len(heads))

    @pl.when((row > 0) & (row % 2 == 0))
    def _():
        greet(me, 0)
        greet(me, row + 1)
        pl.semaphore_wait(barrier, chains - 1 + 2)

    @pl.when(row % 2 == 1)
    def _():
        greet(me, row - 1)
        pl.semaphore_wait(barrier, chains - 1 + 1)

    if rest is not None:
        rest.start()
    own_load.start()

    def send_low(row_to, sem):
        return pltpu.make_async_remote_copy(
            src_ref=low, dst_ref=low, send_sem=xs_send.at[sem], recv_sem=x_recv,
            device_id={"chain": me, "row": row_to}, device_id_type=MESH)

    def send_con(chain_to):
        return pltpu.make_async_remote_copy(
            src_ref=con_out.at[chain_to], dst_ref=con_in.at[me], send_sem=cs_send.at[chain_to],
            recv_sem=c_recv.at[me], device_id={"chain": chain_to, "row": row}, device_id_type=MESH)

    def recv_con(source):
        return pltpu.make_async_remote_copy(
            src_ref=con_out.at[source], dst_ref=con_in.at[source], send_sem=cs_send.at[source],
            recv_sem=c_recv.at[source], device_id={"chain": source, "row": row}, device_id_type=MESH)

    first.wait()

    @pl.when(row == 0)
    def _():
        inv_load.wait()
        inv_high[...] = inv[...].astype(jnp.bfloat16)
        inv_low[...] = (inv[...] - inv_high[...].astype(jnp.float32)).astype(jnp.bfloat16)
        res_load.wait()
        for j in range(chains - 1):
            @pl.when(j < me)
            def _():
                recv_con(j).wait_recv()
                res[...] = res[...] - con_in[j]
        high = res[...].astype(jnp.bfloat16)
        rest_part = (res[...] - high.astype(jnp.float32)).astype(jnp.bfloat16)
        wide = jnp.dot(inv_high[...], jnp.concatenate([high, rest_part], axis=1),
                       preferred_element_type=jnp.float32)
        count = high.shape[1]
        solved = wide[:, :count] + (wide[:, count:] + jnp.dot(
            inv_low[...], high, preferred_element_type=jnp.float32))
        low[...] = solved.astype(jnp.bfloat16)
        for i in range(1, chains):
            @pl.when(i > me)
            def _():
                con_out[i] = scale_ref[i] * jnp.dot(
                    fac[pl.ds(i * tile, tile), :], low[...], preferred_element_type=jnp.float32)
                send_con(i).start()
        for at, r in enumerate(heads):
            send_low(r, at).start()

    @pl.when(row > 0)
    def _():
        send_low(0, 0).wait_recv()

    @pl.when((row > 0) & (row % 2 == 0))
    def _():
        send_low(row + 1, 0).start()

    if rest is not None:
        rest.wait()
    own_load.wait()

    step = min(piece, tile)

    def partial(start, put):
        def body(t, carry):
            at = pl.multiple_of(start + t * step, step)
            index = at // tile
            value = scale_ref[index] * jnp.dot(fac[pl.ds(at, step), :], low[...], preferred_element_type=jnp.float32)
            put(t * step, value)

            @pl.when((row == 0) & (at < window))
            def _():
                keep = jnp.where(index == me, -1.0, 0.0)
                put(t * step, keep * low[pl.ds(at - index * tile, step), :].astype(jnp.float32))
            return carry
        lax.fori_loop(0, piece // step, body, 0)

    def putter(ref, a, s):
        def put(offset, value):
            ref[a, s, pl.ds(offset, step), :] = value.astype(jnp.bfloat16)
        return put

    def message(src, dst, send, recv, a, s):
        return pltpu.make_async_remote_copy(
            src_ref=src.at[a, s], dst_ref=dst.at[a, s], send_sem=send.at[a, s], recv_sem=recv.at[a, s],
            device_id={"chain": peer[a], "row": row}, device_id_type=MESH)

    def received(dst, recv, a, s):
        return pltpu.make_async_remote_copy(
            src_ref=dst.at[a, s], dst_ref=dst.at[a, s], send_sem=recv.at[a, s], recv_sem=recv.at[a, s],
            device_id={"chain": across, "row": row}, device_id_type=MESH)

    def direct_from(a, s):
        return received(dir_in, dir_r, a, s)

    def combined_from(a, s):
        return received(cmb_in, cmb_r, a, s)

    def rel(a, s):
        return message(rel_out, rel_in, rel_s, rel_r, a, s)

    def direct(a, s):
        return message(dir_out, dir_in, dir_s, dir_r, a, s)

    def combined(a, s):
        return message(cmb_out, cmb_in, cmb_s, cmb_r, a, s)

    flying = ([], [])

    def issue(a, copy):
        if len(flying[a]) >= FLIGHT:
            flying[a][-FLIGHT].wait_send()
        copy.start()
        flying[a].append(copy)

    for s in range(SUB):
        for a in range(2):
            partial(across * quarter + (1 - a) * half + s * piece, putter(rel_out, a, s))
            issue(a, rel(a, s))
    for s in range(SUB):
        for a in range(2):
            partial(peer[a] * quarter + (1 - a) * half + s * piece, putter(dir_out, a, s))
            issue(a, direct(a, s))
    for s in range(SUB):
        for a in range(2):
            partial(peer[a] * quarter + a * half + s * piece, putter(cmb_out, a, s))

    @pl.when((row == 0) & (me * quarter < window))
    def _():
        masked = min(quarter, window)

        def wipe(t, carry):
            at = pl.multiple_of(t * step, step)

            @pl.when(me * quarter + at < window)
            def _():
                acc[pl.ds(at, step), :] = jnp.zeros((step, acc.shape[1]), jnp.float32)
            return carry
        lax.fori_loop(0, masked // step, wipe, 0)

    for h in range(2):
        for s in range(SUB):
            base = h * half + s * piece

            def body(t, carry, base=base):
                spot = pl.multiple_of(base + t * step, step)
                at = pl.multiple_of(me * quarter + spot, step)
                index = at // tile
                inside = (row == 0) & (at < window)

                @pl.when(jnp.logical_not(inside))
                def _():
                    acc[pl.ds(spot, step), :] -= scale_ref[index] * jnp.dot(
                        fac[pl.ds(at, step), :], low[...], preferred_element_type=jnp.float32)

                @pl.when(inside & (index == me))
                def _():
                    acc[pl.ds(spot, step), :] = low[pl.ds(at - index * tile, step), :].astype(jnp.float32)
                return carry
            lax.fori_loop(0, piece // step, body, 0)

    def where_is(block, h, s):
        return pl.ds(pl.multiple_of(block * quarter + h * half + s * piece, piece), piece)

    def spread(a, h, s):
        return pltpu.make_async_remote_copy(
            src_ref=own.at[h, s], dst_ref=out_ref.at[where_is(me, h, s)],
            send_sem=ag_s.at[a, h, s], recv_sem=ag_r.at[a, h, s],
            device_id={"chain": peer[a], "row": row}, device_id_type=MESH)

    def arrived(a, h, s):
        return pltpu.make_async_remote_copy(
            src_ref=own.at[h, s], dst_ref=out_ref.at[where_is(peer[a], h, s)],
            send_sem=ag_s.at[a, h, s], recv_sem=ag_r.at[a, h, s],
            device_id={"chain": peer[a], "row": row}, device_id_type=MESH)

    def forward(a, h, s):
        spot = out_ref.at[where_is(peer[a], h, s)]
        return pltpu.make_async_remote_copy(
            src_ref=spot, dst_ref=spot, send_sem=fw_s.at[a, h, s], recv_sem=fw_r.at[a, h, s],
            device_id={"chain": peer[1 - a], "row": row}, device_id_type=MESH)

    def forwarded(a, h, s):
        spot = out_ref.at[where_is(across, h, s)]
        return pltpu.make_async_remote_copy(
            src_ref=spot, dst_ref=spot, send_sem=fw_s.at[a, h, s], recv_sem=fw_r.at[a, h, s],
            device_id={"chain": peer[1 - a], "row": row}, device_id_type=MESH)

    def forwards(a, h):
        return me < 3 if h == a else me == 0

    def is_forwarded(a, h):
        return me != 1 + a if h == a else me == 2 - a

    def keep(h, s):
        return pltpu.make_async_copy(own.at[h, s], out_ref.at[where_is(me, h, s)], own_sem.at[h, s])

    for s in range(SUB):
        for a in range(2):
            rel(1 - a, s).wait_recv()
            cmb_out[a, s] = (cmb_out[a, s].astype(jnp.float32) + rel_in[1 - a, s].astype(jnp.float32)).astype(jnp.bfloat16)
            issue(a, combined(a, s))
    flip = jnp.where(me == 2, 1, 0)
    for k in range(2):
        h = k + (1 - 2 * k) * flip
        for s in range(SUB):
            direct_from(1 - h, s).wait_recv()
            combined_from(h, s).wait_recv()
            own[h, s] = (acc[pl.ds(pl.multiple_of(h * half + s * piece, piece), piece), :]
                         - dir_in[1 - h, s].astype(jnp.float32) - cmb_in[h, s].astype(jnp.float32)).astype(jnp.bfloat16)
            for a in range(2):
                issue(a, spread(a, h, s))
            keep(h, s).start()
    turns = [(a, (k + a) % 2, s) for k in range(2) for s in range(SUB) for a in range(2)]
    for a, h, s in turns:
        arrived(a, h, s).wait_recv()

        @pl.when(forwards(a, h))
        def _():
            forward(a, h, s).start()
    for a, h, s in turns:
        @pl.when(is_forwarded(a, h))
        def _():
            forwarded(a, h, s).wait_recv()

        @pl.when(forwards(a, h))
        def _():
            forward(a, h, s).wait_send()
        if a == 0:
            keep(h, s).wait()
    for a in range(2):
        for copy in flying[a][-FLIGHT:]:
            copy.wait_send()

    @pl.when(row == 0)
    def _():
        for i in range(1, chains):
            @pl.when(i > me)
            def _():
                send_con(i).wait_send()
        for at, r in enumerate(heads):
            send_low(r, at).wait_send()

    @pl.when((row > 0) & (row % 2 == 0))
    def _():
        send_low(row + 1, 0).wait_send()


def local(chains, rows, right_side, factor, tile_scales, diag_inverse):
    local_rows, rhs_count = right_side.shape
    width = factor.shape[2]
    factor = factor.reshape(local_rows, width)
    scales = tile_scales.reshape(-1)
    inverse = diag_inverse.reshape(width, width)
    half = local_rows // 8
    piece = half // SUB
    low = jnp.bfloat16
    pieces = pltpu.VMEM((2, SUB, piece, rhs_count), low)
    sems = pltpu.SemaphoreType.DMA((2, SUB))
    anywhere = pl.BlockSpec(memory_space=pl.ANY)
    heads = len(range(2, rows, 2)) + 1
    gathered = pl.pallas_call(
        functools.partial(kernel, chains, rows),
        out_shape=jax.ShapeDtypeStruct((local_rows, rhs_count), low),
        in_specs=[anywhere, anywhere, pl.BlockSpec(memory_space=pltpu.SMEM), anywhere],
        out_specs=anywhere,
        scratch_shapes=[
            pltpu.VMEM((local_rows, width), low),
            pltpu.VMEM((local_rows // 4, rhs_count), jnp.float32),
            pltpu.VMEM((width, width), jnp.float32),
            pltpu.VMEM((width, width), low),
            pltpu.VMEM((width, width), low),
            pltpu.VMEM((width, rhs_count), jnp.float32),
            pltpu.VMEM((width, rhs_count), low),
            pltpu.VMEM((chains, width, rhs_count), jnp.float32),
            pltpu.VMEM((chains, width, rhs_count), jnp.float32),
            pieces, pieces, pieces, pieces, pieces, pieces, pieces,
            pltpu.SemaphoreType.DMA((5,)),
            pltpu.SemaphoreType.DMA((heads,)),
            pltpu.SemaphoreType.DMA,
            pltpu.SemaphoreType.DMA((chains,)),
            pltpu.SemaphoreType.DMA((chains,)),
            sems, sems, sems, sems, sems, sems,
            pltpu.SemaphoreType.DMA((2, 2, SUB)),
            pltpu.SemaphoreType.DMA((2, 2, SUB)),
            pltpu.SemaphoreType.DMA((2, 2, SUB)),
            pltpu.SemaphoreType.DMA((2, 2, SUB)),
            sems,
        ],
        compiler_params=pltpu.CompilerParams(
            collective_id=0, has_side_effects=True, vmem_limit_bytes=48 * 2**20),
        cost_estimate=pl.CostEstimate(
            flops=2 * local_rows * width * rhs_count, bytes_accessed=2 * local_rows * width, transcendentals=0),
    )(right_side, factor, scales, inverse)
    return gathered.astype(jnp.float32)


def solution(mesh):
    return jax.shard_map(
        functools.partial(local, mesh.shape["chain"], mesh.shape["row"]),
        mesh=mesh,
        in_specs=(
            P("row", None),
            P("row", None, "chain"),
            P("row", None, "chain"),
            P(None, None, "chain"),
        ),
        out_specs=P("row", None),
        check_vma=False,
    )
```
